32 devices in a mesh: hours: 2 (over x), sta: 16 (over z, y, core).
Axes of the slice: x: 2, y: 2, z: 4, core: 2. Of those that a mesh axis runs over, the one named last changes fastest.
Arguments:
- spectra: bfloat16 [32, 32, 4, 2, 2048], P(('hours', 'sta')), parts along dimension 0, may hold values from -60 to 60
- station_counts: int32 [32], P(('hours', 'sta')), parts along dimension 0, may hold values from 16 to 32
- block_pairs: int32 [32, 2], P(('hours', 'sta')), parts along dimension 0, may hold values from 0 to 15, as said below
Outputs:
- correlations: bfloat16 [32, 32, 32, 512], P(('hours', 'sta')), parts along dimension 0
The draws below stay inside these ranges and needn't reach their ends.
There are 2 independent parts, one for each index of `hours`. The reference program is written for one: setup_inputs(seed, part) draws one part's arguments, and reference() takes and returns one part's arrays. A program takes and returns all parts, laid end to end along the dimension named above; each array names one. Nothing has to cross between parts.
Inputs may be any that keep to these rules, and one draw needn't show every extreme that they name: Pair p's row block is held by the device that holds pair p: block_pairs[p, 0] == p; the column block's device, block_pairs[p, 1], differs from it by at most 3, and by exactly 3 for some pairs.
All inputs are finite; a program needn't handle non-finite values.
Results may differ from the reference program's by a relative error of at most 0.0065.
Values may be sent and summed in bfloat16 or wider, within the bound.
A program may use at most 192 MiB of HBM per device.

```python
import math
import jax
import jax.numpy as jnp
from jax import lax

BS = 32
W = 4
BLK_DEV = 1
PAIRS_DEV = 1
F = 2048
LAGS = 512
BAND = 32
REACH = 3
BLOCKS = 16
PAIRS = 16


def draw_spectra(key, part):
    key = jax.random.fold_in(key, 11)
    first_key, second_key = jax.random.split(key)
    full_shape = (BLOCKS, BS, W, 2, F)
    base_values = jnp.clip(jax.random.normal(first_key, full_shape, jnp.float32), -4.0, 4.0)
    spread = math.log(10.0)
    factors = jnp.exp(spread * jax.random.uniform(second_key, (BLOCKS, BS, W, 1, F), jnp.float32))
    return (base_values * factors).astype(jnp.bfloat16)


def draw_block_pairs(key, part):
    key = jax.random.fold_in(key, 23)
    first_key, second_key, third_key = jax.random.split(key, 3)
    devices = BLOCKS // BLK_DEV
    pair_index = jnp.arange(PAIRS, dtype=jnp.int32)
    owner_dev = pair_index // PAIRS_DEV
    row_block = owner_dev * BLK_DEV + jax.random.randint(first_key, (PAIRS,), 0, BLK_DEV, dtype=jnp.int32)
    offsets = jax.random.randint(second_key, (PAIRS,), -REACH, REACH + 1, dtype=jnp.int32)
    edge_offset = jnp.where(owner_dev < devices // 2, REACH, -REACH).astype(jnp.int32)
    at_edge = jnp.logical_and(pair_index % PAIRS_DEV == 0, owner_dev % 4 == 0)
    offsets = jnp.where(at_edge, edge_offset, offsets)
    partner = jnp.clip(owner_dev + offsets, 0, devices - 1)
    column_block = partner * BLK_DEV + jax.random.randint(third_key, (PAIRS,), 0, BLK_DEV, dtype=jnp.int32)
    return jnp.stack([row_block, column_block], axis=1).astype(jnp.int32)


def with_ends(drawn, rng, low, high):
    index_at = [jax.random.randint(jax.random.fold_in(rng, axis), (), 0, length) for axis, length in enumerate(drawn.shape)]
    main_axis = drawn.shape.index(max(drawn.shape))
    next_to = index_at[:main_axis] + [(index_at[main_axis] + 1) % drawn.shape[main_axis]] + index_at[main_axis + 1:]
    return drawn.at[tuple(index_at)].set(low).at[tuple(next_to)].set(high)


def setup_inputs(seed: int = 0, part: int = 0) -> dict:
    key_of = jax.random.split(jax.random.key(seed), 4)
    part_keys = jax.random.split(jax.random.fold_in(key_of[3], part), 4)
    return {
        "spectra": draw_spectra(jax.random.fold_in(jax.random.fold_in(key_of[3], part), 71), part),
        "station_counts": with_ends(jax.random.randint(part_keys[1], (BLOCKS,), BS // 2, BS + 1), jax.random.fold_in(part_keys[1], 1), BS // 2, BS).astype(jnp.int32),
        "block_pairs": draw_block_pairs(jax.random.fold_in(jax.random.fold_in(key_of[3], part), 71), part),
    }


EPSILON = 1e-06

def whiten(spectra, station_counts):
    values = spectra.astype(jnp.float32)
    blocks = values.shape[0]
    stations = values.shape[1]
    windows = values.shape[2]
    freqs = values.shape[4]
    power_sum = lax.optimization_barrier(jnp.sum(values * values, axis=3))
    banded = power_sum.reshape(blocks, stations, windows, freqs // BAND, BAND)
    band_mean = lax.optimization_barrier(jnp.mean(banded, axis=(2, 4)))
    inverse_amp = jnp.repeat(lax.rsqrt(band_mean + EPSILON), BAND, axis=2)
    station_mask = (jnp.arange(stations, dtype=jnp.int32)[None, :] < station_counts[:, None]).astype(jnp.float32)
    weights = inverse_amp * station_mask[:, :, None]
    return (values * weights[:, :, None, None, :]).astype(jnp.bfloat16)

def contract(left, right):
    return jnp.einsum('...iwf,...jwf->...ijf', left, right)

def cross_spectra(first_block, other_block):
    left = first_block.astype(jnp.float32)
    right = other_block.astype(jnp.float32)
    real_part = contract(left[..., 0, :], right[..., 0, :]) + contract(left[..., 1, :], right[..., 1, :])
    imag_part = contract(left[..., 1, :], right[..., 0, :]) - contract(left[..., 0, :], right[..., 1, :])
    return jnp.stack([real_part, imag_part], axis=-2).astype(jnp.bfloat16)

def lag_table(freqs, lags):
    freq_bins = jnp.arange(freqs, dtype=jnp.int32)
    lag_index = jnp.arange(lags, dtype=jnp.int32) - lags // 2
    phase_index = jnp.mod(freq_bins[:, None] * lag_index[None, :], 2 * freqs)
    angles = math.pi / freqs * phase_index.astype(jnp.float32)
    return jnp.concatenate([jnp.cos(angles), -jnp.sin(angles)], axis=0).astype(jnp.bfloat16)

def to_lags(crossed, dft_rows, windows):
    leading = crossed.shape[:-2]
    freqs = crossed.shape[-1]
    flat_rows = crossed.reshape(-1, 2 * freqs)
    summed = jnp.dot(flat_rows.astype(jnp.float32), dft_rows.astype(jnp.float32), preferred_element_type=jnp.float32)
    scaled = summed * (1.0 / math.sqrt(freqs * windows))
    return scaled.reshape(leading + (dft_rows.shape[1],)).astype(jnp.bfloat16)

def reference(spectra, station_counts, block_pairs):
    whitened = whiten(spectra, station_counts)
    dft_rows = lag_table(F, LAGS)

    def one_pair(pair_ids):
        crossed = cross_spectra(whitened[pair_ids[0]], whitened[pair_ids[1]])
        return to_lags(crossed, dft_rows, W)
    return lax.map(one_pair, block_pairs)
```

```python
import functools
import math

import jax
import jax.numpy as jnp
from jax import lax
from jax.experimental import pallas as pl
from jax.experimental.pallas import tpu as pltpu
from jax.sharding import PartitionSpec as P

LAGS = 512
BAND = 32
EPSILON = 1e-06
CHUNK = 256
HALF = LAGS // 2

SIB, MIR, DIAG, SIBMIR, VERT, SIBVERT, OWN = range(7)


def kernel(sta, windows, freqs, counts, pairs, x_ref, out_ref, held, left, right, rows_re, rows_im,
           base, table, acc, sends, recvs):
    chunks = freqs // CHUNK
    parts = 2 * windows
    me = lax.axis_index("sta")
    planes = sta // 4
    plane = me // 4
    odd = lax.rem(me, 2)
    upper = lax.rem(me // 2, 2)
    spot = lax.rem(me, 4)
    inner = jnp.logical_or(spot == 1, spot == 2)
    below = plane > 0
    above = plane < planes - 1
    sibling = me + 1 - 2 * odd
    mirror = me + 2 - 4 * upper
    cross_mirror = me + 3 - 2 * spot
    diag = me - 3 + 6 * odd
    has_diag = jnp.where(odd == 1, above, below)
    up_vert = me + 4 - 8 * upper
    has_up = jnp.where(upper == 1, below, above)
    down_vert = me - 4 + 8 * upper
    has_down = jnp.where(upper == 1, above, below)

    barrier = pltpu.get_barrier_semaphore()

    def greet(other):
        pl.semaphore_signal(barrier, inc=1, device_id={"sta": other}, device_id_type=pl.DeviceIdType.MESH)

    greet(sibling)
    greet(mirror)
    greet(cross_mirror)
    pl.when(has_diag)(lambda: greet(diag))
    pl.when(has_up)(lambda: greet(up_vert))
    pl.when(has_down)(lambda: greet(down_vert))

    def copy(n, source, target, other, number):
        return pltpu.make_async_remote_copy(
            src_ref=held.at[n, source], dst_ref=held.at[n, target],
            send_sem=sends.at[n, number], recv_sem=recvs.at[n, target],
            device_id={"sta": other}, device_id_type=pl.DeviceIdType.MESH)

    def to_sib(n):
        return copy(n, OWN, SIB, sibling, 0)

    def to_mir(n):
        return copy(n, OWN, MIR, mirror, 1)

    def to_diag(n):
        return copy(n, OWN, DIAG, diag, 2)

    def mir_to_sib(n):
        return copy(n, MIR, SIBMIR, sibling, 3)

    def mir_to_vert(n):
        return copy(n, MIR, VERT, up_vert, 4)

    def vert_to_sib(n):
        return copy(n, VERT, SIBVERT, sibling, 5)

    def diag_to_mir(n):
        return copy(n, DIAG, VERT, cross_mirror, 6)

    def turned(n):
        return jnp.logical_and(inner, lax.rem(n, 2) == 1)

    def sends_vert(n):
        return jnp.logical_and(has_up, jnp.logical_not(turned(n)))

    def sends_turned(n):
        return jnp.logical_and(has_diag, turned(n))

    count = counts[0]
    station = lax.broadcasted_iota(jnp.int32, (32, CHUNK), 0)
    mask = jnp.where(station < count, 1.0, 0.0).astype(jnp.float32)
    band_row = lax.broadcasted_iota(jnp.int32, (CHUNK, CHUNK), 0)
    band_col = lax.broadcasted_iota(jnp.int32, (CHUNK, CHUNK), 1)
    same_band = jnp.where(
        jnp.right_shift(band_row, 5) == jnp.right_shift(band_col, 5), 1.0 / (BAND * windows), 0.0
    ).astype(jnp.float32)

    def whiten(n):
        cols = pl.ds(pl.multiple_of(n * CHUNK, CHUNK), CHUNK)
        power = jnp.zeros((32, CHUNK), jnp.float32)
        for part in range(parts):
            value = x_ref[part, :, cols].astype(jnp.float32)
            power += value * value
        mean = jnp.dot(power, same_band, precision=lax.Precision.HIGHEST, preferred_element_type=jnp.float32)
        weight = lax.rsqrt(mean + EPSILON) * mask
        for part in range(parts):
            value = x_ref[part, :, cols].astype(jnp.float32)
            held[n, OWN, part] = (value * weight).astype(jnp.bfloat16)

    def start_own(n):
        whiten(n)
        to_mir(n).start()
        pl.when(has_diag)(lambda: to_diag(n).start())
        to_sib(n).start()

    whiten(0)
    pl.semaphore_wait(
        barrier, 3 + has_diag.astype(jnp.int32) + has_up.astype(jnp.int32) + has_down.astype(jnp.int32))
    to_mir(0).start()
    pl.when(has_diag)(lambda: to_diag(0).start())
    to_sib(0).start()
    start_own(1)
    start_own(2)

    def angle_of(phase):
        period = 4 * freqs
        phase = jnp.bitwise_and(phase, period - 1)
        phase = jnp.where(phase >= period // 2, phase - period, phase)
        return (math.pi / (2 * freqs)) * phase.astype(jnp.float32)

    base_angle = angle_of(band_row * (2 * band_col + 1))
    base[0] = jnp.cos(base_angle)
    base[1] = jnp.sin(base_angle)
    acc[...] = jnp.zeros_like(acc)

    wanted = pairs[0, 1]
    found = {SIB: sibling, MIR: mirror, DIAG: diag, SIBMIR: cross_mirror,
             VERT: me - 2 + 4 * upper, SIBVERT: sibling - 2 + 4 * upper}

    def compute(n):
        lag = lax.broadcasted_iota(jnp.int32, (1, HALF), 1)
        step = angle_of(n * CHUNK * (2 * lag + 1))
        step_cos, step_sin = jnp.cos(step), jnp.sin(step)
        table[0] = (base[0] * step_cos - base[1] * step_sin).astype(jnp.bfloat16)
        table[1] = (base[1] * step_cos + base[0] * step_sin).astype(jnp.bfloat16)
        freq = n * CHUNK + lax.broadcasted_iota(jnp.int32, (1, CHUNK), 1)
        turn = angle_of(freq)
        turn_cos, turn_sin = jnp.cos(turn), jnp.sin(turn)
        for w in range(windows):
            real = held[n, OWN, 2 * w].astype(jnp.float32)
            imag = held[n, OWN, 2 * w + 1].astype(jnp.float32)
            left[2 * w] = real * turn_cos + imag * turn_sin
            left[2 * w + 1] = imag * turn_cos - real * turn_sin
        for part in range(parts):
            value = held[n, OWN, part]
            for kind, block in found.items():
                value = jnp.where(wanted == block, held[n, kind, part], value)
            right[part] = value.astype(jnp.float32)

        def some_rows(g, carry):
            for u in range(8):
                i = g * 8 + u
                re = jnp.zeros((32, CHUNK), jnp.float32)
                im = jnp.zeros((32, CHUNK), jnp.float32)
                for w in range(windows):
                    lr = left[2 * w, pl.ds(i, 1), :]
                    li = left[2 * w + 1, pl.ds(i, 1), :]
                    rr = right[2 * w]
                    ri = right[2 * w + 1]
                    re += lr * rr + li * ri
                    im += li * rr - lr * ri
                rows_re[u * 32:(u + 1) * 32] = re.astype(jnp.bfloat16)
                rows_im[u * 32:(u + 1) * 32] = im.astype(jnp.bfloat16)
            where = pl.ds(pl.multiple_of(g * 256, 256), 256)
            acc[0, where] += jnp.dot(rows_re[...], table[0], preferred_element_type=jnp.float32)
            acc[1, where] += jnp.dot(rows_im[...], table[1], preferred_element_type=jnp.float32)
            return carry

        lax.fori_loop(0, 4, some_rows, 0)

    def vert_arrives(n):
        return jnp.where(turned(n), has_down, has_down)

    def one_step(n, carry):
        @pl.when(n < chunks)
        def _():
            to_mir(n).wait_recv()
            pl.when(sends_vert(n))(lambda: mir_to_vert(n).start())
            mir_to_sib(n).start()
            pl.when(has_diag)(lambda: to_diag(n).wait_recv())
            pl.when(sends_turned(n))(lambda: diag_to_mir(n).start())

        @pl.when(n + 3 < chunks)
        def _():
            start_own(n + 3)

        @pl.when(jnp.logical_and(n >= 1, n <= chunks))
        def _():
            @pl.when(has_down)
            def _():
                mir_to_vert(n - 1).wait_recv()
                vert_to_sib(n - 1).start()

        @pl.when(n >= 2)
        def _():
            m = n - 2
            to_sib(m).wait_recv()
            mir_to_sib(m).wait_recv()
            pl.when(has_down)(lambda: vert_to_sib(m).wait_recv())
            compute(m)
        return carry

    lax.fori_loop(0, chunks + 2, one_step, 0)

    def finish(n, carry):
        to_sib(n).wait_send()
        to_mir(n).wait_send()
        pl.when(has_diag)(lambda: to_diag(n).wait_send())
        mir_to_sib(n).wait_send()
        pl.when(sends_vert(n))(lambda: mir_to_vert(n).wait_send())
        pl.when(has_down)(lambda: vert_to_sib(n).wait_send())
        pl.when(sends_turned(n))(lambda: diag_to_mir(n).wait_send())
        return carry

    lax.fori_loop(0, chunks, finish, 0)

    scale = 1.0 / math.sqrt(freqs * windows)
    flip = jnp.where(band_row + band_col == HALF - 1, 1.0, 0.0).astype(jnp.bfloat16)

    def write(g, carry):
        where = pl.ds(pl.multiple_of(g * 256, 256), 256)
        even, odd_part = acc[0, where], acc[1, where]
        out_ref[where, HALF:] = ((even - odd_part) * scale).astype(jnp.bfloat16)
        mirrored = ((even + odd_part) * scale).astype(jnp.bfloat16)
        out_ref[where, :HALF] = jnp.dot(mirrored, flip, preferred_element_type=jnp.float32).astype(jnp.bfloat16)
        return carry

    lax.fori_loop(0, 4, write, 0)


def local(sta, spectra, station_counts, block_pairs):
    _, stations, windows, two, freqs = spectra.shape
    chunks = freqs // CHUNK
    parts = two * windows
    arranged = jnp.transpose(spectra.reshape(stations, parts, freqs), (1, 0, 2))
    out = pl.pallas_call(
        functools.partial(kernel, sta, windows, freqs),
        out_shape=jax.ShapeDtypeStruct((stations * stations, LAGS), jnp.bfloat16),
        in_specs=[
            pl.BlockSpec(memory_space=pltpu.SMEM),
            pl.BlockSpec(memory_space=pltpu.SMEM),
            pl.BlockSpec(memory_space=pltpu.VMEM),
        ],
        out_specs=pl.BlockSpec(memory_space=pltpu.VMEM),
        scratch_shapes=[
            pltpu.VMEM((chunks, 7, parts, stations, CHUNK), jnp.bfloat16),
            pltpu.VMEM((parts, stations, CHUNK), jnp.float32),
            pltpu.VMEM((parts, stations, CHUNK), jnp.float32),
            pltpu.VMEM((256, CHUNK), jnp.bfloat16),
            pltpu.VMEM((256, CHUNK), jnp.bfloat16),
            pltpu.VMEM((2, CHUNK, HALF), jnp.float32),
            pltpu.VMEM((2, CHUNK, HALF), jnp.bfloat16),
            pltpu.VMEM((2, stations * stations, HALF), jnp.float32),
            pltpu.SemaphoreType.DMA((chunks, 7)),
            pltpu.SemaphoreType.DMA((chunks, 6)),
        ],
        compiler_params=pltpu.CompilerParams(
            collective_id=0, has_side_effects=True, vmem_limit_bytes=40 * 1024 * 1024),
    )(station_counts, block_pairs, arranged)
    return out.reshape(1, stations, stations, LAGS)


def solution(mesh):
    placed = (
        P(("hours", "sta"), None, None, None, None),
        P(("hours", "sta")),
        P(("hours", "sta"), None),
    )
    return jax.shard_map(
        functools.partial(local, mesh.shape["sta"]),
        mesh=mesh,
        in_specs=placed,
        out_specs=P(("hours", "sta"), None, None, None),
        check_vma=False,
    )
```

```python
import functools
import math

import jax
import jax.numpy as jnp
from jax import lax
from jax.experimental import pallas as pl
from jax.experimental.pallas import tpu as pltpu
from jax.sharding import PartitionSpec as P

LAGS = 512
BAND = 32
EPSILON = 1e-06
CHUNK = 256
AHEAD = 4
HALF = LAGS // 2

SIB, MIR, DIAG, SIBMIR, VERT, PICK, OWN = range(7)


def kernel(sta, windows, freqs, counts, pairs, x_ref, out_ref, held, left, right, rows_re, rows_im,
           base, table, acc, my_want, their_want, sends, recvs, want_sems):
    chunks = freqs // CHUNK
    parts = 2 * windows
    me = lax.axis_index("sta")
    planes = sta // 4
    plane = me // 4
    odd = lax.rem(me, 2)
    upper = lax.rem(me // 2, 2)
    spot = lax.rem(me, 4)
    inner = jnp.logical_or(spot == 1, spot == 2)
    below = plane > 0
    above = plane < planes - 1
    sibling = me + 1 - 2 * odd
    mirror = me + 2 - 4 * upper
    cross_mirror = me + 3 - 2 * spot
    diag = me - 3 + 6 * odd
    diag_out = jnp.logical_and(jnp.logical_not(inner), jnp.where(odd == 1, above, below))
    diag_in = jnp.logical_and(inner, jnp.where(odd == 1, above, below))
    has_diag = jnp.logical_or(diag_out, diag_in)
    up_vert = me + 4 - 8 * upper
    has_up = jnp.where(upper == 1, below, above)
    down_vert = me - 4 + 8 * upper
    has_down = jnp.where(upper == 1, above, below)

    barrier = pltpu.get_barrier_semaphore()

    def greet(other):
        pl.semaphore_signal(barrier, inc=1, device_id={"sta": other}, device_id_type=pl.DeviceIdType.MESH)

    greet(sibling)
    greet(mirror)
    pl.when(has_diag)(lambda: greet(diag))
    pl.when(has_up)(lambda: greet(up_vert))
    pl.when(has_down)(lambda: greet(down_vert))

    def copy(n, source, target, other, number):
        return pltpu.make_async_remote_copy(
            src_ref=held.at[n, source], dst_ref=held.at[n, target],
            send_sem=sends.at[n, number], recv_sem=recvs.at[n, target],
            device_id={"sta": other}, device_id_type=pl.DeviceIdType.MESH)

    def to_sib(n):
        return copy(n, OWN, SIB, sibling, 0)

    def to_mir(n):
        return copy(n, OWN, MIR, mirror, 1)

    def to_diag(n):
        return copy(n, OWN, DIAG, diag, 2)

    def mir_to_sib(n):
        return copy(n, MIR, SIBMIR, sibling, 3)

    def pick_to_vert(n):
        return copy(n, PICK, VERT, up_vert, 4)

    def want_copy():
        return pltpu.make_async_remote_copy(
            src_ref=my_want, dst_ref=their_want, send_sem=want_sems.at[0], recv_sem=want_sems.at[1],
            device_id={"sta": down_vert}, device_id_type=pl.DeviceIdType.MESH)

    count = counts[0]
    station = lax.broadcasted_iota(jnp.int32, (32, CHUNK), 0)
    mask = jnp.where(station < count, 1.0, 0.0).astype(jnp.float32)
    band_row = lax.broadcasted_iota(jnp.int32, (CHUNK, CHUNK), 0)
    band_col = lax.broadcasted_iota(jnp.int32, (CHUNK, CHUNK), 1)
    same_band = jnp.where(
        jnp.right_shift(band_row, 5) == jnp.right_shift(band_col, 5), 1.0 / (BAND * windows), 0.0
    ).astype(jnp.float32)

    def whiten(n):
        cols = pl.ds(pl.multiple_of(n * CHUNK, CHUNK), CHUNK)
        power = jnp.zeros((32, CHUNK), jnp.float32)
        for part in range(parts):
            value = x_ref[part, :, cols].astype(jnp.float32)
            power += value * value
        mean = jnp.dot(power, same_band, precision=lax.Precision.HIGHEST, preferred_element_type=jnp.float32)
        weight = lax.rsqrt(mean + EPSILON) * mask
        for part in range(parts):
            value = x_ref[part, :, cols].astype(jnp.float32)
            held[n, OWN, part] = (value * weight).astype(jnp.bfloat16)

    def start_own(n):
        whiten(n)
        to_mir(n).start()
        pl.when(diag_out)(lambda: to_diag(n).start())
        to_sib(n).start()

    wanted = pairs[0, 1]
    my_want[...] = jnp.full_like(my_want, wanted.astype(jnp.float32))
    whiten(0)
    pl.semaphore_wait(
        barrier, 2 + has_diag.astype(jnp.int32) + has_up.astype(jnp.int32) + has_down.astype(jnp.int32))
    to_mir(0).start()
    pl.when(diag_out)(lambda: to_diag(0).start())
    to_sib(0).start()
    pl.when(has_down)(lambda: want_copy().start())
    for n in range(1, AHEAD):
        start_own(n)

    def angle_of(phase):
        period = 4 * freqs
        phase = jnp.bitwise_and(phase, period - 1)
        phase = jnp.where(phase >= period // 2, phase - period, phase)
        return (math.pi / (2 * freqs)) * phase.astype(jnp.float32)

    base_angle = angle_of(band_row * (2 * band_col + 1))
    base[0] = jnp.cos(base_angle)
    base[1] = jnp.sin(base_angle)
    acc[...] = jnp.zeros_like(acc)

    from_vert = jnp.where(upper == 1, wanted >= 4 * plane + 4, wanted < 4 * plane)
    found = ((SIB, wanted == sibling), (MIR, wanted == mirror), (SIBMIR, wanted == cross_mirror),
             (DIAG, jnp.logical_and(inner, wanted == diag)), (VERT, from_vert))

    def compute(n):
        lag = lax.broadcasted_iota(jnp.int32, (1, HALF), 1)
        step = angle_of(n * CHUNK * (2 * lag + 1))
        step_cos, step_sin = jnp.cos(step), jnp.sin(step)
        table[0] = (base[0] * step_cos - base[1] * step_sin).astype(jnp.bfloat16)
        table[1] = (base[1] * step_cos + base[0] * step_sin).astype(jnp.bfloat16)
        freq = n * CHUNK + lax.broadcasted_iota(jnp.int32, (1, CHUNK), 1)
        turn = angle_of(freq)
        turn_cos, turn_sin = jnp.cos(turn), jnp.sin(turn)
        for w in range(windows):
            real = held[n, OWN, 2 * w].astype(jnp.float32)
            imag = held[n, OWN, 2 * w + 1].astype(jnp.float32)
            left[2 * w] = real * turn_cos + imag * turn_sin
            left[2 * w + 1] = imag * turn_cos - real * turn_sin
        for part in range(parts):
            value = held[n, OWN, part]
            for kind, is_it in found:
                value = jnp.where(is_it, held[n, kind, part], value)
            right[part] = value.astype(jnp.float32)

        def some_rows(g, carry):
            for u in range(8):
                i = g * 8 + u
                re = jnp.zeros((32, CHUNK), jnp.float32)
                im = jnp.zeros((32, CHUNK), jnp.float32)
                for w in range(windows):
                    lr = left[2 * w, pl.ds(i, 1), :]
                    li = left[2 * w + 1, pl.ds(i, 1), :]
                    rr = right[2 * w]
                    ri = right[2 * w + 1]
                    re += lr * rr + li * ri
                    im += li * rr - lr * ri
                rows_re[u * 32:(u + 1) * 32] = re.astype(jnp.bfloat16)
                rows_im[u * 32:(u + 1) * 32] = im.astype(jnp.bfloat16)
            where = pl.ds(pl.multiple_of(g * 256, 256), 256)
            acc[0, where] += jnp.dot(rows_re[...], table[0], preferred_element_type=jnp.float32)
            acc[1, where] += jnp.dot(rows_im[...], table[1], preferred_element_type=jnp.float32)
            return carry

        lax.fori_loop(0, 4, some_rows, 0)

    pl.when(has_up)(lambda: want_copy().wait_recv())
    above_wants = jnp.max(their_want[...])
    picks_mirror = above_wants == mirror.astype(jnp.float32)
    picks_cross = above_wants == cross_mirror.astype(jnp.float32)

    def pick(n):
        for part in range(parts):
            value = jnp.where(picks_mirror, held[n, MIR, part], held[n, SIB, part])
            held[n, PICK, part] = jnp.where(picks_cross, held[n, SIBMIR, part], value)

    def one_step(n, carry):
        @pl.when(n < chunks)
        def _():
            to_mir(n).wait_recv()
            mir_to_sib(n).start()

        @pl.when(n + AHEAD < chunks)
        def _():
            start_own(n + AHEAD)

        @pl.when(n >= 2)
        def _():
            m = n - 2
            pl.when(diag_in)(lambda: to_diag(m).wait_recv())
            pl.when(has_down)(lambda: pick_to_vert(m).wait_recv())
            compute(m)

        @pl.when(n < chunks)
        def _():
            to_sib(n).wait_recv()
            mir_to_sib(n).wait_recv()

            @pl.when(has_up)
            def _():
                pick(n)
                pick_to_vert(n).start()
        return carry

    lax.fori_loop(0, chunks + 2, one_step, 0)

    def finish(n, carry):
        to_sib(n).wait_send()
        to_mir(n).wait_send()
        pl.when(diag_out)(lambda: to_diag(n).wait_send())
        mir_to_sib(n).wait_send()
        pl.when(has_up)(lambda: pick_to_vert(n).wait_send())
        return carry

    lax.fori_loop(0, chunks, finish, 0)
    pl.when(has_down)(lambda: want_copy().wait_send())

    scale = 1.0 / math.sqrt(freqs * windows)
    flip = jnp.where(band_row + band_col == HALF - 1, 1.0, 0.0).astype(jnp.bfloat16)

    def write(g, carry):
        where = pl.ds(pl.multiple_of(g * 256, 256), 256)
        even, odd_part = acc[0, where], acc[1, where]
        out_ref[where, HALF:] = ((even - odd_part) * scale).astype(jnp.bfloat16)
        mirrored = ((even + odd_part) * scale).astype(jnp.bfloat16)
        out_ref[where, :HALF] = jnp.dot(mirrored, flip, preferred_element_type=jnp.float32).astype(jnp.bfloat16)
        return carry

    lax.fori_loop(0, 4, write, 0)


def local(sta, spectra, station_counts, block_pairs):
    _, stations, windows, two, freqs = spectra.shape
    chunks = freqs // CHUNK
    parts = two * windows
    arranged = jnp.transpose(spectra.reshape(stations, parts, freqs), (1, 0, 2))
    out = pl.pallas_call(
        functools.partial(kernel, sta, windows, freqs),
        out_shape=jax.ShapeDtypeStruct((stations * stations, LAGS), jnp.bfloat16),
        in_specs=[
            pl.BlockSpec(memory_space=pltpu.SMEM),
            pl.BlockSpec(memory_space=pltpu.SMEM),
            pl.BlockSpec(memory_space=pltpu.VMEM),
        ],
        out_specs=pl.BlockSpec(memory_space=pltpu.VMEM),
        scratch_shapes=[
            pltpu.VMEM((chunks, 7, parts, stations, CHUNK), jnp.bfloat16),
            pltpu.VMEM((parts, stations, CHUNK), jnp.float32),
            pltpu.VMEM((parts, stations, CHUNK), jnp.float32),
            pltpu.VMEM((256, CHUNK), jnp.bfloat16),
            pltpu.VMEM((256, CHUNK), jnp.bfloat16),
            pltpu.VMEM((2, CHUNK, HALF), jnp.float32),
            pltpu.VMEM((2, CHUNK, HALF), jnp.bfloat16),
            pltpu.VMEM((2, stations * stations, HALF), jnp.float32),
            pltpu.VMEM((8, 128), jnp.float32),
            pltpu.VMEM((8, 128), jnp.float32),
            pltpu.SemaphoreType.DMA((chunks, 5)),
            pltpu.SemaphoreType.DMA((chunks, 5)),
            pltpu.SemaphoreType.DMA((2,)),
        ],
        compiler_params=pltpu.CompilerParams(
            collective_id=0, has_side_effects=True, vmem_limit_bytes=40 * 1024 * 1024),
    )(station_counts, block_pairs, arranged)
    return out.reshape(1, stations, stations, LAGS)


def solution(mesh):
    placed = (
        P(("hours", "sta"), None, None, None, None),
        P(("hours", "sta")),
        P(("hours", "sta"), None),
    )
    return jax.shard_map(
        functools.partial(local, mesh.shape["sta"]),
        mesh=mesh,
        in_specs=placed,
        out_specs=P(("hours", "sta"), None, None, None),
        check_vma=False,
    )
```

```python
import functools
import math

import jax
import jax.numpy as jnp
from jax import lax
from jax.experimental import pallas as pl
from jax.experimental.pallas import tpu as pltpu
from jax.sharding import PartitionSpec as P

LAGS = 512
BAND = 32
EPSILON = 1e-06
CHUNK = 256
AHEAD = 4
HALF = LAGS // 2

SIB, MIR, DIAG, SIBMIR, VERT, PICK, OWN = range(7)


def kernel(sta, windows, freqs, counts, pairs, x_ref, out_ref, held, left, right, rows_re, rows_im,
           base, table, acc, my_want, their_want, sends, recvs, want_sems):
    chunks = freqs // CHUNK
    parts = 2 * windows
    me = lax.axis_index("sta")
    planes = sta // 4
    plane = me // 4
    odd = lax.rem(me, 2)
    upper = lax.rem(me // 2, 2)
    spot = lax.rem(me, 4)
    inner = jnp.logical_or(spot == 1, spot == 2)
    below = plane > 0
    above = plane < planes - 1
    sibling = me + 1 - 2 * odd
    mirror = me + 2 - 4 * upper
    cross_mirror = me + 3 - 2 * spot
    diag = me - 3 + 6 * odd
    diag_out = jnp.logical_and(jnp.logical_not(inner), jnp.where(odd == 1, above, below))
    diag_in = jnp.logical_and(inner, jnp.where(odd == 1, above, below))
    has_diag = jnp.logical_or(diag_out, diag_in)
    up_vert = me + 4 - 8 * upper
    has_up = jnp.where(upper == 1, below, above)
    down_vert = me - 4 + 8 * upper
    has_down = jnp.where(upper == 1, above, below)

    barrier = pltpu.get_barrier_semaphore()

    def greet(other):
        pl.semaphore_signal(barrier, inc=1, device_id={"sta": other}, device_id_type=pl.DeviceIdType.MESH)

    greet(sibling)
    greet(mirror)
    pl.when(has_diag)(lambda: greet(diag))
    pl.when(has_up)(lambda: greet(up_vert))
    pl.when(has_down)(lambda: greet(down_vert))

    def copy(n, source, target, other, number):
        return pltpu.make_async_remote_copy(
            src_ref=held.at[n, source], dst_ref=held.at[n, target],
            send_sem=sends.at[n, number], recv_sem=recvs.at[n, target],
            device_id={"sta": other}, device_id_type=pl.DeviceIdType.MESH)

    def to_sib(n):
        return copy(n, OWN, SIB, sibling, 0)

    def to_mir(n):
        return copy(n, OWN, MIR, mirror, 1)

    def to_diag(n):
        return copy(n, OWN, DIAG, diag, 2)

    def mir_to_sib(n):
        return copy(n, MIR, SIBMIR, sibling, 3)

    def pick_to_vert(n):
        return copy(n, PICK, VERT, up_vert, 4)

    def want_copy():
        return pltpu.make_async_remote_copy(
            src_ref=my_want, dst_ref=their_want, send_sem=want_sems.at[0], recv_sem=want_sems.at[1],
            device_id={"sta": down_vert}, device_id_type=pl.DeviceIdType.MESH)

    count = counts[0]
    station = lax.broadcasted_iota(jnp.int32, (32, CHUNK), 0)
    mask = jnp.where(station < count, 1.0, 0.0).astype(jnp.float32)
    band_row = lax.broadcasted_iota(jnp.int32, (CHUNK, CHUNK), 0)
    band_col = lax.broadcasted_iota(jnp.int32, (CHUNK, CHUNK), 1)
    same_band = jnp.where(
        jnp.right_shift(band_row, 5) == jnp.right_shift(band_col, 5), 1.0 / (BAND * windows), 0.0
    ).astype(jnp.bfloat16)

    def whiten(n):
        cols = pl.ds(pl.multiple_of(n * CHUNK, CHUNK), CHUNK)
        power = jnp.zeros((32, CHUNK), jnp.float32)
        for part in range(parts):
            value = x_ref[part, :, cols].astype(jnp.float32)
            power += value * value
        high = power.astype(jnp.bfloat16)
        low = (power - high.astype(jnp.float32)).astype(jnp.bfloat16)
        mean = jnp.dot(high, same_band, preferred_element_type=jnp.float32)
        mean += jnp.dot(low, same_band, preferred_element_type=jnp.float32)
        weight = lax.rsqrt(mean + EPSILON) * mask
        for part in range(parts):
            value = x_ref[part, :, cols].astype(jnp.float32)
            held[n, OWN, part] = (value * weight).astype(jnp.bfloat16)

    def start_own(n):
        whiten(n)
        to_mir(n).start()
        pl.when(diag_out)(lambda: to_diag(n).start())
        to_sib(n).start()

    wanted = pairs[0, 1]
    my_want[...] = jnp.full_like(my_want, wanted.astype(jnp.float32))
    whiten(0)
    pl.semaphore_wait(
        barrier, 2 + has_diag.astype(jnp.int32) + has_up.astype(jnp.int32) + has_down.astype(jnp.int32))
    to_mir(0).start()
    pl.when(diag_out)(lambda: to_diag(0).start())
    to_sib(0).start()
    pl.when(has_down)(lambda: want_copy().start())
    for n in range(1, AHEAD):
        start_own(n)

    def angle_of(phase):
        period = 4 * freqs
        phase = jnp.bitwise_and(phase, period - 1)
        phase = jnp.where(phase >= period // 2, phase - period, phase)
        return (math.pi / (2 * freqs)) * phase.astype(jnp.float32)

    coarse = lax.broadcasted_iota(jnp.int32, (16, HALF), 0)
    twice = 2 * lax.broadcasted_iota(jnp.int32, (16, HALF), 1) + 1
    coarse_angle, fine_angle = angle_of(16 * coarse * twice), angle_of(coarse * twice)
    coarse_cos, coarse_sin = jnp.cos(coarse_angle), jnp.sin(coarse_angle)
    fine_cos, fine_sin = jnp.cos(fine_angle), jnp.sin(fine_angle)
    for a in range(CHUNK // 16):
        cos_a, sin_a = coarse_cos[a:a + 1], coarse_sin[a:a + 1]
        base[0, a * 16:a * 16 + 16] = cos_a * fine_cos - sin_a * fine_sin
        base[1, a * 16:a * 16 + 16] = sin_a * fine_cos + cos_a * fine_sin
    acc[...] = jnp.zeros_like(acc)

    from_vert = jnp.where(upper == 1, wanted >= 4 * plane + 4, wanted < 4 * plane)
    found = ((SIB, wanted == sibling), (MIR, wanted == mirror), (SIBMIR, wanted == cross_mirror),
             (DIAG, jnp.logical_and(inner, wanted == diag)), (VERT, from_vert))

    def compute(n):
        lag = lax.broadcasted_iota(jnp.int32, (1, HALF), 1)
        step = angle_of(n * CHUNK * (2 * lag + 1))
        step_cos, step_sin = jnp.cos(step), jnp.sin(step)
        table[0] = (base[0] * step_cos - base[1] * step_sin).astype(jnp.bfloat16)
        table[1] = (base[1] * step_cos + base[0] * step_sin).astype(jnp.bfloat16)
        freq = n * CHUNK + lax.broadcasted_iota(jnp.int32, (1, CHUNK), 1)
        turn = angle_of(freq)
        turn_cos, turn_sin = jnp.cos(turn), jnp.sin(turn)
        for w in range(windows):
            real = held[n, OWN, 2 * w].astype(jnp.float32)
            imag = held[n, OWN, 2 * w + 1].astype(jnp.float32)
            left[2 * w] = real * turn_cos + imag * turn_sin
            left[2 * w + 1] = imag * turn_cos - real * turn_sin
        for part in range(parts):
            value = held[n, OWN, part]
            for kind, is_it in found:
                value = jnp.where(is_it, held[n, kind, part], value)
            right[part] = value.astype(jnp.float32)

        def some_rows(g, carry):
            for u in range(8):
                i = g * 8 + u
                re = jnp.zeros((32, CHUNK), jnp.float32)
                im = jnp.zeros((32, CHUNK), jnp.float32)
                for w in range(windows):
                    lr = left[2 * w, pl.ds(i, 1), :]
                    li = left[2 * w + 1, pl.ds(i, 1), :]
                    rr = right[2 * w]
                    ri = right[2 * w + 1]
                    re += lr * rr + li * ri
                    im += li * rr - lr * ri
                rows_re[u * 32:(u + 1) * 32] = re.astype(jnp.bfloat16)
                rows_im[u * 32:(u + 1) * 32] = im.astype(jnp.bfloat16)
            where = pl.ds(pl.multiple_of(g * 256, 256), 256)
            acc[0, where] += jnp.dot(rows_re[...], table[0], preferred_element_type=jnp.float32)
            acc[1, where] += jnp.dot(rows_im[...], table[1], preferred_element_type=jnp.float32)
            return carry

        lax.fori_loop(0, 4, some_rows, 0)

    pl.when(has_up)(lambda: want_copy().wait_recv())
    above_wants = jnp.max(their_want[...])
    picks_mirror = above_wants == mirror.astype(jnp.float32)
    picks_cross = above_wants == cross_mirror.astype(jnp.float32)

    def pick(n):
        for part in range(parts):
            value = jnp.where(picks_mirror, held[n, MIR, part], held[n, SIB, part])
            held[n, PICK, part] = jnp.where(picks_cross, held[n, SIBMIR, part], value)

    def one_step(n, carry):
        @pl.when(n < chunks)
        def _():
            to_mir(n).wait_recv()
            mir_to_sib(n).start()

        @pl.when(n + AHEAD < chunks)
        def _():
            start_own(n + AHEAD)

        @pl.when(n < chunks)
        def _():
            to_sib(n).wait_recv()
            mir_to_sib(n).wait_recv()

            @pl.when(has_up)
            def _():
                pick(n)
                pick_to_vert(n).start()

        @pl.when(n >= 2)
        def _():
            m = n - 2
            pl.when(diag_in)(lambda: to_diag(m).wait_recv())
            pl.when(has_down)(lambda: pick_to_vert(m).wait_recv())
            compute(m)

        return carry

    lax.fori_loop(0, chunks + 2, one_step, 0)

    def finish(n, carry):
        to_sib(n).wait_send()
        to_mir(n).wait_send()
        pl.when(diag_out)(lambda: to_diag(n).wait_send())
        mir_to_sib(n).wait_send()
        pl.when(has_up)(lambda: pick_to_vert(n).wait_send())
        return carry

    lax.fori_loop(0, chunks, finish, 0)
    pl.when(has_down)(lambda: want_copy().wait_send())

    scale = 1.0 / math.sqrt(freqs * windows)
    flip = jnp.where(band_row + band_col == HALF - 1, 1.0, 0.0).astype(jnp.bfloat16)

    def write(g, carry):
        where = pl.ds(pl.multiple_of(g * 256, 256), 256)
        even, odd_part = acc[0, where], acc[1, where]
        out_ref[where, HALF:] = ((even - odd_part) * scale).astype(jnp.bfloat16)
        mirrored = ((even + odd_part) * scale).astype(jnp.bfloat16)
        out_ref[where, :HALF] = jnp.dot(mirrored, flip, preferred_element_type=jnp.float32).astype(jnp.bfloat16)
        return carry

    lax.fori_loop(0, 4, write, 0)


def local(sta, spectra, station_counts, block_pairs):
    _, stations, windows, two, freqs = spectra.shape
    chunks = freqs // CHUNK
    parts = two * windows
    arranged = jnp.transpose(spectra.reshape(stations, parts, freqs), (1, 0, 2))
    out = pl.pallas_call(
        functools.partial(kernel, sta, windows, freqs),
        out_shape=jax.ShapeDtypeStruct((stations * stations, LAGS), jnp.bfloat16),
        in_specs=[
            pl.BlockSpec(memory_space=pltpu.SMEM),
            pl.BlockSpec(memory_space=pltpu.SMEM),
            pl.BlockSpec(memory_space=pltpu.VMEM),
        ],
        out_specs=pl.BlockSpec(memory_space=pltpu.VMEM),
        scratch_shapes=[
            pltpu.VMEM((chunks, 7, parts, stations, CHUNK), jnp.bfloat16),
            pltpu.VMEM((parts, stations, CHUNK), jnp.float32),
            pltpu.VMEM((parts, stations, CHUNK), jnp.float32),
            pltpu.VMEM((256, CHUNK), jnp.bfloat16),
            pltpu.VMEM((256, CHUNK), jnp.bfloat16),
            pltpu.VMEM((2, CHUNK, HALF), jnp.float32),
            pltpu.VMEM((2, CHUNK, HALF), jnp.bfloat16),
            pltpu.VMEM((2, stations * stations, HALF), jnp.float32),
            pltpu.VMEM((8, 128), jnp.float32),
            pltpu.VMEM((8, 128), jnp.float32),
            pltpu.SemaphoreType.DMA((chunks, 5)),
            pltpu.SemaphoreType.DMA((chunks, 5)),
            pltpu.SemaphoreType.DMA((2,)),
        ],
        compiler_params=pltpu.CompilerParams(
            collective_id=0, has_side_effects=True, vmem_limit_bytes=40 * 1024 * 1024),
    )(station_counts, block_pairs, arranged)
    return out.reshape(1, stations, stations, LAGS)


def solution(mesh):
    placed = (
        P(("hours", "sta"), None, None, None, None),
        P(("hours", "sta")),
        P(("hours", "sta"), None),
    )
    return jax.shard_map(
        functools.partial(local, mesh.shape["sta"]),
        mesh=mesh,
        in_specs=placed,
        out_specs=P(("hours", "sta"), None, None, None),
        check_vma=False,
    )
```

```python
import functools
import math

import jax
import jax.numpy as jnp
from jax import lax
from jax.experimental import pallas as pl
from jax.experimental.pallas import tpu as pltpu
from jax.sharding import PartitionSpec as P

LAGS = 512
BAND = 32
EPSILON = 1e-06
CHUNK = 256
AHEAD = 4
HALF = LAGS // 2

SIB, MIR, DIAG, SIBMIR, VERT, PICK, OWN = range(7)


def kernel(sta, windows, freqs, counts, pairs, x_ref, out_ref, held, left, right, rows_re, rows_im,
           base, table, acc, my_want, their_want, sends, recvs, want_sems):
    chunks = freqs // CHUNK
    parts = 2 * windows
    me = lax.axis_index("sta")
    planes = sta // 4
    plane = me // 4
    odd = lax.rem(me, 2)
    upper = lax.rem(me // 2, 2)
    spot = lax.rem(me, 4)
    inner = jnp.logical_or(spot == 1, spot == 2)
    below = plane > 0
    above = plane < planes - 1
    sibling = me + 1 - 2 * odd
    mirror = me + 2 - 4 * upper
    cross_mirror = me + 3 - 2 * spot
    diag = me - 3 + 6 * odd
    diag_out = jnp.logical_and(jnp.logical_not(inner), jnp.where(odd == 1, above, below))
    diag_in = jnp.logical_and(inner, jnp.where(odd == 1, above, below))
    has_diag = jnp.logical_or(diag_out, diag_in)
    up_vert = me + 4 - 8 * upper
    has_up = jnp.where(upper == 1, below, above)
    down_vert = me - 4 + 8 * upper
    has_down = jnp.where(upper == 1, above, below)

    barrier = pltpu.get_barrier_semaphore()

    def greet(other):
        pl.semaphore_signal(barrier, inc=1, device_id={"sta": other}, device_id_type=pl.DeviceIdType.MESH)

    greet(sibling)
    greet(mirror)
    pl.when(has_diag)(lambda: greet(diag))
    pl.when(has_up)(lambda: greet(up_vert))
    pl.when(has_down)(lambda: greet(down_vert))

    def copy(n, source, target, other, number):
        return pltpu.make_async_remote_copy(
            src_ref=held.at[n, source], dst_ref=held.at[n, target],
            send_sem=sends.at[n, number], recv_sem=recvs.at[n, target],
            device_id={"sta": other}, device_id_type=pl.DeviceIdType.MESH)

    def to_sib(n):
        return copy(n, OWN, SIB, sibling, 0)

    def to_mir(n):
        return copy(n, OWN, MIR, mirror, 1)

    def to_diag(n):
        return copy(n, OWN, DIAG, diag, 2)

    def mir_to_sib(n):
        return copy(n, MIR, SIBMIR, sibling, 3)

    def pick_to_vert(n):
        return copy(n, PICK, VERT, up_vert, 4)

    def want_copy():
        return pltpu.make_async_remote_copy(
            src_ref=my_want, dst_ref=their_want, send_sem=want_sems.at[0], recv_sem=want_sems.at[1],
            device_id={"sta": down_vert}, device_id_type=pl.DeviceIdType.MESH)

    count = counts[0]
    station = lax.broadcasted_iota(jnp.int32, (32, CHUNK), 0)
    mask = jnp.where(station < count, 1.0, 0.0).astype(jnp.float32)
    band_row = lax.broadcasted_iota(jnp.int32, (CHUNK, CHUNK), 0)
    band_col = lax.broadcasted_iota(jnp.int32, (CHUNK, CHUNK), 1)
    same_band = jnp.where(
        jnp.right_shift(band_row, 5) == jnp.right_shift(band_col, 5), 1.0 / (BAND * windows), 0.0
    ).astype(jnp.bfloat16)

    def whiten(n):
        cols = pl.ds(pl.multiple_of(n * CHUNK, CHUNK), CHUNK)
        power = jnp.zeros((32, CHUNK), jnp.float32)
        for part in range(parts):
            value = x_ref[part, :, cols].astype(jnp.float32)
            power += value * value
        high = power.astype(jnp.bfloat16)
        low = (power - high.astype(jnp.float32)).astype(jnp.bfloat16)
        mean = jnp.dot(high, same_band, preferred_element_type=jnp.float32)
        mean += jnp.dot(low, same_band, preferred_element_type=jnp.float32)
        weight = lax.rsqrt(mean + EPSILON) * mask
        for part in range(parts):
            value = x_ref[part, :, cols].astype(jnp.float32)
            held[n, OWN, part] = (value * weight).astype(jnp.bfloat16)

    def start_own(n):
        whiten(n)
        to_mir(n).start()
        pl.when(diag_out)(lambda: to_diag(n).start())
        to_sib(n).start()

    wanted = pairs[0, 1]
    my_want[...] = jnp.full_like(my_want, wanted.astype(jnp.float32))
    whiten(0)
    pl.semaphore_wait(
        barrier, 2 + has_diag.astype(jnp.int32) + has_up.astype(jnp.int32) + has_down.astype(jnp.int32))
    to_mir(0).start()
    pl.when(diag_out)(lambda: to_diag(0).start())
    to_sib(0).start()
    pl.when(has_down)(lambda: want_copy().start())
    for n in range(1, AHEAD):
        start_own(n)

    def angle_of(phase):
        period = 4 * freqs
        phase = jnp.bitwise_and(phase, period - 1)
        phase = jnp.where(phase >= period // 2, phase - period, phase)
        return (math.pi / (2 * freqs)) * phase.astype(jnp.float32)

    coarse = lax.broadcasted_iota(jnp.int32, (16, HALF), 0)
    twice = 2 * lax.broadcasted_iota(jnp.int32, (16, HALF), 1) + 1
    coarse_angle, fine_angle = angle_of(16 * coarse * twice), angle_of(coarse * twice)
    coarse_cos, coarse_sin = jnp.cos(coarse_angle), jnp.sin(coarse_angle)
    fine_cos, fine_sin = jnp.cos(fine_angle), jnp.sin(fine_angle)
    for a in range(CHUNK // 16):
        cos_a, sin_a = coarse_cos[a:a + 1], coarse_sin[a:a + 1]
        base[0, a * 16:a * 16 + 16] = cos_a * fine_cos - sin_a * fine_sin
        base[1, a * 16:a * 16 + 16] = sin_a * fine_cos + cos_a * fine_sin
    acc[...] = jnp.zeros_like(acc)

    from_vert = jnp.where(upper == 1, wanted >= 4 * plane + 4, wanted < 4 * plane)
    found = ((SIB, wanted == sibling), (MIR, wanted == mirror), (SIBMIR, wanted == cross_mirror),
             (DIAG, jnp.logical_and(inner, wanted == diag)), (VERT, from_vert))

    def compute(n):
        lag = lax.broadcasted_iota(jnp.int32, (1, HALF), 1)
        step = angle_of(n * CHUNK * (2 * lag + 1))
        step_cos, step_sin = jnp.cos(step), jnp.sin(step)
        table[0] = (base[0] * step_cos - base[1] * step_sin).astype(jnp.bfloat16)
        table[1] = (base[1] * step_cos + base[0] * step_sin).astype(jnp.bfloat16)
        freq = n * CHUNK + lax.broadcasted_iota(jnp.int32, (1, CHUNK), 1)
        turn = angle_of(freq)
        turn_cos, turn_sin = jnp.cos(turn), jnp.sin(turn)
        for w in range(windows):
            real = held[n, OWN, 2 * w].astype(jnp.float32)
            imag = held[n, OWN, 2 * w + 1].astype(jnp.float32)
            turned_real = real * turn_cos + imag * turn_sin
            turned_imag = imag * turn_cos - real * turn_sin
            left[2 * w] = turned_real
            left[2 * w + 1] = turned_imag
            left[parts + w] = turned_real + turned_imag
        for part in range(parts):
            value = held[n, OWN, part]
            for kind, is_it in found:
                value = jnp.where(is_it, held[n, kind, part], value)
            right[part] = value.astype(jnp.float32)
        for w in range(windows):
            right[parts + w] = right[2 * w] - right[2 * w + 1]

        def some_rows(g, carry):
            for u in range(8):
                i = g * 8 + u
                both_re = both_im = mixed = None
                for w in range(windows):
                    lr = left[2 * w, pl.ds(i, 1), :]
                    li = left[2 * w + 1, pl.ds(i, 1), :]
                    ls = left[parts + w, pl.ds(i, 1), :]
                    a, b, c = lr * right[2 * w], li * right[2 * w + 1], ls * right[parts + w]
                    both_re = a if w == 0 else both_re + a
                    both_im = b if w == 0 else both_im + b
                    mixed = c if w == 0 else mixed + c
                re = both_re + both_im
                im = mixed - both_re + both_im
                rows_re[u * 32:(u + 1) * 32] = re.astype(jnp.bfloat16)
                rows_im[u * 32:(u + 1) * 32] = im.astype(jnp.bfloat16)
            where = pl.ds(pl.multiple_of(g * 256, 256), 256)
            acc[0, where] += jnp.dot(rows_re[...], table[0], preferred_element_type=jnp.float32)
            acc[1, where] += jnp.dot(rows_im[...], table[1], preferred_element_type=jnp.float32)
            return carry

        lax.fori_loop(0, 4, some_rows, 0)

    pl.when(has_up)(lambda: want_copy().wait_recv())
    above_wants = jnp.max(their_want[...])
    picks_mirror = above_wants == mirror.astype(jnp.float32)
    picks_cross = above_wants == cross_mirror.astype(jnp.float32)

    def pick(n):
        for part in range(parts):
            value = jnp.where(picks_mirror, held[n, MIR, part], held[n, SIB, part])
            held[n, PICK, part] = jnp.where(picks_cross, held[n, SIBMIR, part], value)

    def one_step(n, carry):
        @pl.when(n < chunks)
        def _():
            to_mir(n).wait_recv()
            mir_to_sib(n).start()

        @pl.when(n + AHEAD < chunks)
        def _():
            start_own(n + AHEAD)

        @pl.when(n < chunks)
        def _():
            to_sib(n).wait_recv()
            mir_to_sib(n).wait_recv()

            @pl.when(has_up)
            def _():
                pick(n)
                pick_to_vert(n).start()

        @pl.when(n >= 2)
        def _():
            m = n - 2
            pl.when(diag_in)(lambda: to_diag(m).wait_recv())
            pl.when(has_down)(lambda: pick_to_vert(m).wait_recv())
            compute(m)

        return carry

    lax.fori_loop(0, chunks + 2, one_step, 0)

    def finish(n, carry):
        to_sib(n).wait_send()
        to_mir(n).wait_send()
        pl.when(diag_out)(lambda: to_diag(n).wait_send())
        mir_to_sib(n).wait_send()
        pl.when(has_up)(lambda: pick_to_vert(n).wait_send())
        return carry

    lax.fori_loop(0, chunks, finish, 0)
    pl.when(has_down)(lambda: want_copy().wait_send())

    scale = 1.0 / math.sqrt(freqs * windows)
    flip = jnp.where(band_row + band_col == HALF - 1, 1.0, 0.0).astype(jnp.bfloat16)

    def write(g, carry):
        where = pl.ds(pl.multiple_of(g * 256, 256), 256)
        even, odd_part = acc[0, where], acc[1, where]
        out_ref[where, HALF:] = ((even - odd_part) * scale).astype(jnp.bfloat16)
        mirrored = ((even + odd_part) * scale).astype(jnp.bfloat16)
        out_ref[where, :HALF] = jnp.dot(mirrored, flip, preferred_element_type=jnp.float32).astype(jnp.bfloat16)
        return carry

    lax.fori_loop(0, 4, write, 0)


def local(sta, spectra, station_counts, block_pairs):
    _, stations, windows, two, freqs = spectra.shape
    chunks = freqs // CHUNK
    parts = two * windows
    arranged = jnp.transpose(spectra.reshape(stations, parts, freqs), (1, 0, 2))
    out = pl.pallas_call(
        functools.partial(kernel, sta, windows, freqs),
        out_shape=jax.ShapeDtypeStruct((stations * stations, LAGS), jnp.bfloat16),
        in_specs=[
            pl.BlockSpec(memory_space=pltpu.SMEM),
            pl.BlockSpec(memory_space=pltpu.SMEM),
            pl.BlockSpec(memory_space=pltpu.VMEM),
        ],
        out_specs=pl.BlockSpec(memory_space=pltpu.VMEM),
        scratch_shapes=[
            pltpu.VMEM((chunks, 7, parts, stations, CHUNK), jnp.bfloat16),
            pltpu.VMEM((parts + windows, stations, CHUNK), jnp.float32),
            pltpu.VMEM((parts + windows, stations, CHUNK), jnp.float32),
            pltpu.VMEM((256, CHUNK), jnp.bfloat16),
            pltpu.VMEM((256, CHUNK), jnp.bfloat16),
            pltpu.VMEM((2, CHUNK, HALF), jnp.float32),
            pltpu.VMEM((2, CHUNK, HALF), jnp.bfloat16),
            pltpu.VMEM((2, stations * stations, HALF), jnp.float32),
            pltpu.VMEM((8, 128), jnp.float32),
            pltpu.VMEM((8, 128), jnp.float32),
            pltpu.SemaphoreType.DMA((chunks, 5)),
            pltpu.SemaphoreType.DMA((chunks, 5)),
            pltpu.SemaphoreType.DMA((2,)),
        ],
        compiler_params=pltpu.CompilerParams(
            collective_id=0, has_side_effects=True, vmem_limit_bytes=40 * 1024 * 1024),
    )(station_counts, block_pairs, arranged)
    return out.reshape(1, stations, stations, LAGS)


def solution(mesh):
    placed = (
        P(("hours", "sta"), None, None, None, None),
        P(("hours", "sta")),
        P(("hours", "sta"), None),
    )
    return jax.shard_map(
        functools.partial(local, mesh.shape["sta"]),
        mesh=mesh,
        in_specs=placed,
        out_specs=P(("hours", "sta"), None, None, None),
        check_vma=False,
    )
```
